256 devices in a mesh: dev: 128 (over x_lo, y, z, core), rep: 2 (over x_hi).
Axes of the slice: x: 4 (x_hi: 2, x_lo: 2; x = x_hi * 2 + x_lo), y: 4, z: 8, core: 2. Of those that a mesh axis runs over, the one named last changes fastest.
Arguments:
- pair_state: bfloat16 [512, 512, 128], P('dev', 'rep'), may hold values from -6 to 6
- token_pair_mask: int32 [512, 512], P('dev', 'rep'), may hold values 0 or 1
- alignment_state: bfloat16 [128, 512, 64], P('rep', 'dev'), may hold values from -6 to 6
- alignment_mask: int32 [128, 512], P('rep', 'dev'), may hold values 0 or 1
- input_weight: bfloat16 [128, 640], replicated, may hold values from -0.5 to 0.5
- output_weight: bfloat16 [128, 128], replicated, may hold values from -0.5 to 0.5
- alignment_weight: bfloat16 [64, 64], replicated, may hold values from -0.75 to 0.75
- outer_weight: bfloat16 [1024, 128], replicated, may hold values from -1 to 1
Outputs:
- pair_new: bfloat16 [512, 512, 128], P('dev', 'rep')
The draws below stay inside these ranges and needn't reach their ends.
All inputs are finite; a program needn't handle non-finite values. No bound on the sum of `token_pair_mask` or of `alignment_mask` on one device may be relied on, other than what follows from the above.
Results may differ from the reference program's by a relative error of at most 0.011.
Values may be sent and summed in bfloat16 or wider, within the bound.
No kernel may reach another device: no remote copies, remote signals or barrier semaphores. Data moves between devices by JAX's collectives and lax.ppermute only.
A program may use at most 64 MiB of HBM per device.

```python
import jax
import jax.numpy as jnp
from jax import lax

PAIR_WIDTH = 128
ALIGNMENT_WIDTH = 64
FACTOR_WIDTH = 32
ALIGNMENT_ROWS = 128
TOKEN_COUNT = 512


def plant(entries, key, least, top_value):
    spot = [jax.random.randint(jax.random.fold_in(key, axis), (), 0, length) for axis, length in enumerate(entries.shape)]
    widest = entries.shape.index(max(entries.shape))
    next_to = spot[:widest] + [(spot[widest] + 1) % entries.shape[widest]] + spot[widest + 1:]
    return entries.at[tuple(spot)].set(least).at[tuple(next_to)].set(top_value)


def level_of(own_key, extent, split, low, top_value):
    def one(position, blocks):
        heights = jax.random.uniform(jax.random.fold_in(jax.random.fold_in(own_key, 6), position), (blocks,), jnp.float32, low / len(split), top_value / len(split))
        return jnp.repeat(jnp.exp(heights), extent[position] // blocks).reshape((-1,) + (1,) * (len(extent) - position - 1))

    gain = one(*split[0])
    for cut in split[1:]:
        gain = gain * one(*cut)
    return gain


def noise(stream_key, shape, scale, bound, split=(), dtype=jnp.bfloat16):
    loudness = level_of(stream_key, shape, split, -0.22, 0.18) if split else 1.0
    drawn = jax.random.normal(stream_key, shape, jnp.float32) * scale * loudness
    return jnp.minimum(jnp.maximum(drawn, -bound), bound).astype(dtype)


def setup_inputs(seed: int = 0) -> dict:
    key_of = jax.random.split(jax.random.key(seed), 9)
    return {
        "pair_state": noise(key_of[0], (TOKEN_COUNT, TOKEN_COUNT, PAIR_WIDTH), 1.0, 6.0, ((0, 128), (1, 2))),
        "token_pair_mask": plant((jax.random.randint(key_of[1], (TOKEN_COUNT, TOKEN_COUNT), 0, 8) < 7).astype(jnp.int32), jax.random.fold_in(key_of[1], 1), 0, 1),
        "alignment_state": noise(key_of[2], (ALIGNMENT_ROWS, TOKEN_COUNT, ALIGNMENT_WIDTH), 1.0, 6.0, ((0, 2), (1, 128))),
        "alignment_mask": plant((jax.random.randint(key_of[3], (ALIGNMENT_ROWS, TOKEN_COUNT), 0, 4) < 3).astype(jnp.int32), jax.random.fold_in(key_of[3], 1), 0, 1),
        "input_weight": noise(key_of[4], (PAIR_WIDTH, 5 * PAIR_WIDTH), PAIR_WIDTH ** -0.5, 0.5),
        "output_weight": noise(key_of[5], (PAIR_WIDTH, PAIR_WIDTH), PAIR_WIDTH ** -0.5, 0.5),
        "alignment_weight": noise(key_of[6], (ALIGNMENT_WIDTH, 2 * FACTOR_WIDTH), ALIGNMENT_WIDTH ** -0.5, 0.75),
        "outer_weight": noise(key_of[7], (FACTOR_WIDTH * FACTOR_WIDTH, PAIR_WIDTH), (max(4096 // ALIGNMENT_ROWS, 1)) ** -0.5, 1.0),
    }


def apply_layer_norm(values):
    center = lax.optimization_barrier(jnp.mean(values, axis=-1, keepdims=True))
    spread = lax.optimization_barrier(jnp.mean((values - center) ** 2, axis=-1, keepdims=True))
    return (values - center) * lax.rsqrt(spread + 1e-05)

def reference(pair_state, token_pair_mask, alignment_state, alignment_mask, input_weight, output_weight, alignment_weight, outer_weight):
    valid_count = TOKEN_COUNT
    width = PAIR_WIDTH
    state = pair_state.astype(jnp.float32)
    normed = apply_layer_norm(state).astype(jnp.bfloat16).reshape(valid_count * valid_count, width)

    def project(index):
        part = jnp.dot(normed, input_weight[:, index * width:(index + 1) * width], preferred_element_type=jnp.float32)
        return part.reshape(valid_count, valid_count, width)
    maskf = token_pair_mask.astype(jnp.float32)[:, :, None]
    left = (jax.nn.sigmoid(project(0)) * project(1) * maskf).astype(jnp.bfloat16)
    right = (jax.nn.sigmoid(project(2)) * project(3) * maskf).astype(jnp.bfloat16)
    gate = jax.nn.sigmoid(project(4))
    left_t = jnp.transpose(left, (2, 0, 1))
    right_t = jnp.transpose(right, (2, 0, 1))

    def channel_product(operands):
        return jnp.dot(operands[0], operands[1].T, preferred_element_type=jnp.float32).astype(jnp.bfloat16)
    tri_sum = lax.map(channel_product, (left_t, right_t))
    tri_norm = apply_layer_norm(jnp.transpose(tri_sum, (1, 2, 0)).astype(jnp.float32)).astype(jnp.bfloat16)
    tri_out = gate * jnp.dot(tri_norm.reshape(valid_count * valid_count, width), output_weight, preferred_element_type=jnp.float32).reshape(valid_count, valid_count, width)
    alignment_normed = apply_layer_norm(alignment_state.astype(jnp.float32)).astype(jnp.bfloat16)
    alignment_projected = jnp.dot(alignment_normed.reshape(ALIGNMENT_ROWS * valid_count, ALIGNMENT_WIDTH), alignment_weight, preferred_element_type=jnp.float32).reshape(ALIGNMENT_ROWS, valid_count, 2 * FACTOR_WIDTH)
    alignment_mask_float = alignment_mask.astype(jnp.float32)[:, :, None]
    factor_left = (alignment_projected[:, :, :FACTOR_WIDTH] * alignment_mask_float).astype(jnp.bfloat16)
    factor_right = (alignment_projected[:, :, FACTOR_WIDTH:] * alignment_mask_float).astype(jnp.bfloat16)
    trunk_blocks = jnp.transpose(factor_left.reshape(ALIGNMENT_ROWS, valid_count // 8, 8, FACTOR_WIDTH), (1, 0, 2, 3))
    opm_weight = outer_weight.astype(jnp.float32)
    right_factor = factor_right.astype(jnp.float32)

    def block_outer(trunk_block):
        outer_mean = jnp.einsum('zrm,zla->rlam', trunk_block.astype(jnp.float32), right_factor) / ALIGNMENT_ROWS
        flattened = outer_mean.reshape(8 * valid_count, FACTOR_WIDTH * FACTOR_WIDTH)
        return jnp.dot(flattened, opm_weight, precision=lax.Precision.HIGHEST).reshape(8, valid_count, width)
    opm_out = lax.map(block_outer, trunk_blocks).reshape(valid_count, valid_count, width)
    return (state + opm_out + tri_out).astype(jnp.bfloat16)
```

```python
import jax
import jax.numpy as jnp
from jax import lax
from jax.sharding import Mesh, PartitionSpec as P

FACTOR_WIDTH = 32
ALIGNMENT_ROWS = 128
DEV = ("xl", "y", "z", "c")
PLANE = ("xl", "y", "c", "xh")
ALL = ("xl", "y", "z", "c", "xh")


def apply_layer_norm(values, axis):
    center = jnp.mean(values, axis=axis, keepdims=True)
    spread = jnp.mean((values - center) ** 2, axis=axis, keepdims=True)
    return (values - center) * lax.rsqrt(spread + 1e-05)


def factors(alignment_state, alignment_mask, alignment_weight):
    normed = apply_layer_norm(alignment_state.astype(jnp.float32), -1).astype(jnp.bfloat16)
    maskf = alignment_mask.astype(jnp.float32)
    fac_a = jnp.einsum(
        "szm,mc->zsc", normed, alignment_weight[:, :FACTOR_WIDTH], preferred_element_type=jnp.float32
    )
    fac_b = jnp.einsum(
        "szm,md->zds", normed, alignment_weight[:, FACTOR_WIDTH:], preferred_element_type=jnp.float32
    )
    fac_a = (fac_a * maskf.T[:, :, None]).astype(jnp.bfloat16)
    fac_b = (fac_b * maskf.T[:, None, :]).astype(jnp.bfloat16)
    return fac_a, fac_b


def shards(
    pair_state,
    token_pair_mask,
    alignment_state,
    alignment_mask,
    input_weight,
    output_weight,
    alignment_weight,
    outer_weight,
):
    rows, half, width = pair_state.shape
    points = rows * half
    seqs, _, _ = alignment_state.shape
    sizes = {name: lax.axis_size(name) for name in ALL}
    ny, nz, nc, nr = sizes["y"], sizes["z"], sizes["c"], sizes["xh"]
    devs = sizes["xl"] * ny * nz * nc
    depth = FACTOR_WIDTH * seqs

    fac_a, fac_b = factors(alignment_state, alignment_mask, alignment_weight)
    piece = fac_b.reshape(1, rows, depth)
    peers = sizes["xl"] * ny * nc * nr
    plane = lax.all_to_all(
        jnp.broadcast_to(piece, (peers, rows, depth)), PLANE, split_axis=0, concat_axis=0, tiled=True
    )
    plane = plane.reshape(sizes["xl"], ny, nc, nr, rows, depth)
    plane = lax.dynamic_index_in_dim(plane, lax.axis_index("xh"), 0, keepdims=False)
    plane = jnp.transpose(plane, (0, 1, 3, 2, 4)).reshape(ny * nc * rows, nr * depth)
    gathered = lax.all_gather(plane, "z", axis=0, tiled=True)
    other_a = lax.ppermute(fac_a, "xh", [(i, (i + 1) % nr) for i in range(nr)])
    first = lax.axis_index("xh") == 0
    both_a = jnp.stack([jnp.where(first, fac_a, other_a), jnp.where(first, other_a, fac_a)], 1)
    terms = jnp.einsum(
        "irsc,dcf->rdsif",
        both_a,
        outer_weight.reshape(FACTOR_WIDTH, FACTOR_WIDTH, width),
        preferred_element_type=jnp.float32,
    ) * (1.0 / ALIGNMENT_ROWS)
    terms = terms.astype(jnp.bfloat16).reshape(nr * depth, rows * width)

    state = pair_state.reshape(points, width).astype(jnp.float32)
    normed = apply_layer_norm(state, -1).astype(jnp.bfloat16)
    stacked = jnp.einsum(
        "pc,cf->fp", normed, input_weight[:, : 4 * width], preferred_element_type=jnp.float32
    ).reshape(2, 2, width, points)
    maskf = token_pair_mask.reshape(1, 1, points).astype(jnp.float32)
    pair_factors = (jax.nn.sigmoid(stacked[:, 0]) * stacked[:, 1] * maskf).astype(jnp.bfloat16)
    pair_factors = jnp.transpose(pair_factors.reshape(2, width, rows, half), (1, 0, 2, 3))
    pair_factors = pair_factors.reshape(width, 2 * rows, half)
    gate = jax.nn.sigmoid(
        jnp.dot(normed, input_weight[:, 4 * width :], preferred_element_type=jnp.float32)
    )
    swapped = lax.all_to_all(pair_factors, DEV, split_axis=0, concat_axis=0, tiled=True)
    swapped = swapped.reshape(devs, 2, rows, half)
    left = swapped[:, 0].reshape(devs * rows, half)
    right = swapped[:, 1].reshape(devs * rows, half)
    partial = lax.dot_general(
        left, right, (((1,), (1,)), ((), ())), preferred_element_type=jnp.float32
    ).astype(jnp.bfloat16)
    partial = jnp.transpose(partial.reshape(devs, rows, nr, half), (0, 2, 1, 3))
    back = lax.all_to_all(
        partial.reshape(devs * nr, rows, half), ALL, split_axis=0, concat_axis=0, tiled=True
    )
    back = back.reshape(devs, nr, points).astype(jnp.float32)
    tri_sum = (back[:, 0] + back[:, 1]).astype(jnp.bfloat16).astype(jnp.float32)
    tri_norm = apply_layer_norm(tri_sum, 0).astype(jnp.bfloat16)
    tri_out = gate * jnp.einsum(
        "cp,cd->pd", tri_norm, output_weight, preferred_element_type=jnp.float32
    )
    opm = jnp.dot(gathered, terms, preferred_element_type=jnp.float32)
    opm = opm.reshape(nz, ny, nc * rows, rows, width)
    opm = jnp.transpose(opm, (3, 1, 0, 2, 4)).reshape(points, width)
    return (state + opm + tri_out).astype(jnp.bfloat16).reshape(rows, half, width)


def solution(mesh):
    grid = Mesh(mesh.devices.reshape(2, 4, 8, 2, 2), ALL)
    inner = jax.shard_map(
        shards,
        mesh=grid,
        in_specs=(
            P(DEV, "xh", None),
            P(DEV, "xh"),
            P("xh", DEV, None),
            P("xh", DEV),
            P(),
            P(),
            P(),
            P(),
        ),
        out_specs=P(DEV, "xh", None),
        check_vma=False,
    )
    return inner
```

```python
import functools

import jax
import jax.numpy as jnp
from jax import lax
from jax.experimental import pallas as pl
from jax.experimental.pallas import tpu as pltpu
from jax.sharding import Mesh, PartitionSpec as P

FACTOR_WIDTH = 32
ALIGNMENT_ROWS = 128
VMEM_LIMIT = 56 * 1024 * 1024
PROJECT_LIMIT = 56 * 1024 * 1024
DEV = ("xl", "y", "z", "c")
PLANE = ("xl", "y", "c", "xh")
ALL = ("xl", "y", "z", "c", "xh")


def apply_layer_norm(values, axis):
    center = jnp.mean(values, axis=axis, keepdims=True)
    spread = jnp.mean((values - center) ** 2, axis=axis, keepdims=True)
    return (values - center) * lax.rsqrt(spread + 1e-05)


def normalize(values):
    values = values - jnp.mean(values, axis=-1, keepdims=True)
    spread = jnp.mean(values * values, axis=-1, keepdims=True)
    return values * lax.rsqrt(spread + 1e-05)


def factors_kernel(align_ref, align_mask_ref, align_weight_ref, first_ref, second_ref):
    seqs, tokens, _ = align_ref.shape
    align = jnp.swapaxes(align_ref[...].astype(jnp.float32), 0, 1)
    columns = [normalize(align[tok]) for tok in range(tokens)]
    both = lax.dot_general(
        align_weight_ref[...],
        jnp.concatenate(columns, 0).astype(jnp.bfloat16),
        (((0,), (1,)), ((), ())),
        preferred_element_type=jnp.float32,
    )
    align_mask = align_mask_ref[...].astype(jnp.float32)
    tiles = []
    for tok in range(tokens):
        part = both[:, tok * seqs : (tok + 1) * seqs] * align_mask[tok : tok + 1, :]
        first_ref[:, tok * seqs : (tok + 1) * seqs] = part[:FACTOR_WIDTH].astype(jnp.bfloat16)
        part = part[FACTOR_WIDTH:]
        tiles.append(jnp.concatenate([part[: FACTOR_WIDTH // 2], part[FACTOR_WIDTH // 2 :]], 1))
    second_ref[...] = jnp.swapaxes(jnp.stack(tiles), 0, 1).astype(jnp.bfloat16)


def factors(align, align_mask, align_weight):
    seqs, tokens, _ = align.shape
    return pl.pallas_call(
        factors_kernel,
        out_shape=(
            jax.ShapeDtypeStruct((FACTOR_WIDTH, tokens * seqs), jnp.bfloat16),
            jax.ShapeDtypeStruct((FACTOR_WIDTH // 2, tokens, 2 * seqs), jnp.bfloat16),
        ),
        compiler_params=pltpu.CompilerParams(vmem_limit_bytes=VMEM_LIMIT),
        name="factors",
    )(align, align_mask.T, align_weight)


def project_kernel(state_ref, mask_ref, weight_ref, out_ref):
    rows, half, width = state_ref.shape
    weight = weight_ref[:, : 4 * width]
    for row in range(rows):
        normed = normalize(state_ref[row].astype(jnp.float32)).astype(jnp.bfloat16)
        stacked = lax.dot_general(
            weight, normed, (((0,), (1,)), ((), ())), preferred_element_type=jnp.float32
        )
        maskf = mask_ref[row : row + 1, :].astype(jnp.float32)
        for side in range(2):
            opened = stacked[2 * side * width : (2 * side + 1) * width]
            linear = stacked[(2 * side + 1) * width : (2 * side + 2) * width]
            factor = jax.nn.sigmoid(opened) * linear * maskf
            out_ref[row, :, side * half : (side + 1) * half] = factor.astype(jnp.bfloat16)


def project(pair_state, mask, weight):
    rows, half, width = pair_state.shape
    return pl.pallas_call(
        project_kernel,
        out_shape=jax.ShapeDtypeStruct((rows, width, 2 * half), jnp.bfloat16),
        compiler_params=pltpu.CompilerParams(vmem_limit_bytes=PROJECT_LIMIT),
        name="project",
    )(pair_state, mask, weight)


def pack_kernel(grid, factor_ref, second_ref, send_ref):
    nx, ny, nz, nc = grid
    slices, tokens, lanes = second_ref.shape
    sides = factor_ref.shape[2]
    send_ref[:, :, :sides] = jnp.swapaxes(factor_ref[...].astype(jnp.float32), 0, 1).astype(jnp.bfloat16)
    pieces = second_ref[...].astype(jnp.float32).reshape(1, ny, 1, 2, nc, tokens, lanes)
    pieces = jnp.broadcast_to(pieces, (nx, ny, nz // 2, 2, nc, tokens, lanes))
    send_ref[:, :, sides:] = pieces.reshape(nx * ny * nz * nc, tokens, lanes).astype(jnp.bfloat16)


def pack(grid, factor, second):
    rows, width, sides = factor.shape
    return pl.pallas_call(
        functools.partial(pack_kernel, grid),
        out_shape=jax.ShapeDtypeStruct((width, rows, sides + second.shape[2]), jnp.bfloat16),
        compiler_params=pltpu.CompilerParams(vmem_limit_bytes=32 * 1024 * 1024),
        name="pack",
    )(factor, second)


def gate_kernel(state_ref, weight_ref, out_ref):
    values = state_ref[...].astype(jnp.float32)
    values = values - jnp.mean(values, axis=-1, keepdims=True)
    spread = jnp.mean(values * values, axis=-1, keepdims=True)
    normed = (values * lax.rsqrt(spread + 1e-05)).astype(jnp.bfloat16)
    out_ref[...] = jax.nn.sigmoid(
        jnp.dot(normed, weight_ref[:, 4 * state_ref.shape[1] :], preferred_element_type=jnp.float32)
    )


def gates(state, weight):
    return pl.pallas_call(
        gate_kernel,
        out_shape=jax.ShapeDtypeStruct(state.shape, jnp.float32),
        name="gates",
    )(state, weight)


def terms_kernel(place_ref, first_ref, weight_ref, out_ref):
    ny, nc, parts, rows = 4, 2, 2, 4
    columns = first_ref.shape[1] // parts
    width = weight_ref.shape[1]
    seqs = columns // rows
    own, came = first_ref[:, :columns], first_ref[:, columns:]
    mine = place_ref[2] == 0
    spread = jnp.concatenate([jnp.where(mine, own, came), jnp.where(mine, came, own)], 1)
    for core in range(nc):
        for turn in range(ny):
            for flip in range(2):
                piece = lax.rem(place_ref[0] + ny - turn, ny) * 2 + lax.rem(place_ref[3] + flip, 2)
                piece = piece * nc + lax.rem(place_ref[1] + core, nc)
                pair = [
                    weight_ref[pl.ds((dh * FACTOR_WIDTH // 2 + piece) * FACTOR_WIDTH, FACTOR_WIDTH), :]
                    for dh in range(2)
                ]
                product = lax.dot_general(
                    spread, jnp.concatenate(pair, 1), (((0,), (0,)), ((), ())), preferred_element_type=jnp.float32
                ).astype(jnp.bfloat16)
                for part in range(parts):
                    for row in range(rows):
                        start = part * columns + row * seqs
                        for dh in range(2):
                            at = ((((core * ny + turn) * 2 + flip) * parts + part) * 2 + dh) * seqs
                            out_ref[at : at + seqs, row * width : (row + 1) * width] = product[
                                start : start + seqs, dh * width : (dh + 1) * width
                            ]


def outer_terms(place, first, weight, rows):
    columns = first.shape[1]
    depth = FACTOR_WIDTH * columns // rows
    width = weight.shape[1]
    return pl.pallas_call(
        terms_kernel,
        in_specs=[
            pl.BlockSpec(memory_space=pltpu.SMEM),
            pl.BlockSpec(memory_space=pltpu.VMEM),
            pl.BlockSpec(memory_space=pltpu.VMEM),
        ],
        out_shape=jax.ShapeDtypeStruct((depth, rows * width), jnp.bfloat16),
        cost_estimate=pl.CostEstimate(
            flops=2 * depth * rows * width * FACTOR_WIDTH, bytes_accessed=2 * depth * rows * width, transcendentals=0
        ),
        compiler_params=pltpu.CompilerParams(vmem_limit_bytes=32 * 1024 * 1024),
        name="outer_terms",
    )(place, first, weight)


def compact(values):
    groups, rows, lanes = values.shape
    pairs = values.reshape(groups // 2, 2, rows, lanes)
    return jnp.concatenate([pairs[:, 0], pairs[:, 1]], 1).reshape(groups * rows, lanes)


def partial_kernel(swapped_ref, out_ref, table_ref):
    devs, rows, lanes = swapped_ref.shape
    parts = 2
    half = out_ref.shape[2]
    values = compact(swapped_ref[...].astype(jnp.float32))
    left = values[:, :half].astype(jnp.bfloat16)
    right = values[:, half : 2 * half].astype(jnp.bfloat16)
    for part in range(parts):
        product = lax.dot_general(
            left,
            right[part * half : (part + 1) * half],
            (((1,), (1,)), ((), ())),
            preferred_element_type=jnp.float32,
        )
        product = product.reshape(devs // 2, 2 * rows, half)
        product = jnp.stack([product[:, :rows], product[:, rows:]], 1).reshape(devs, rows, half)
        out_ref[part * devs : (part + 1) * devs] = product.astype(jnp.bfloat16)
    table = [values[part * half : (part + 1) * half, 2 * half :] for part in range(parts)]
    table_ref[...] = jnp.concatenate(table, 1).astype(jnp.bfloat16)


def partials(swapped, half):
    devs, rows, lanes = swapped.shape
    return pl.pallas_call(
        partial_kernel,
        out_shape=(
            jax.ShapeDtypeStruct((2 * devs, rows, half), jnp.bfloat16),
            jax.ShapeDtypeStruct((half, 2 * (lanes - 2 * half)), jnp.bfloat16),
        ),
        compiler_params=pltpu.CompilerParams(vmem_limit_bytes=32 * 1024 * 1024),
        name="partials",
    )(swapped)


def shards(
    pair_state,
    token_pair_mask,
    alignment_state,
    alignment_mask,
    input_weight,
    output_weight,
    alignment_weight,
    outer_weight,
):
    rows, half, width = pair_state.shape
    points = rows * half
    sizes = [lax.axis_size(name) for name in ALL]
    nx, ny, nz, nc, nr = sizes
    seqs = alignment_state.shape[0]
    devs = nx * ny * nz * nc
    place = jnp.stack([lax.axis_index(name) for name in ("y", "c", "xh", "z")])
    place = place.astype(jnp.int32) % jnp.array([ny, nc, nr, 2], jnp.int32)

    fac_a, fac_b = factors(alignment_state, alignment_mask, alignment_weight)
    fac_b = lax.ppermute(fac_b, ("xl", "xh"), [(0, 0), (1, 2), (2, 1), (3, 3)])
    swap = [(0, 1), (1, 0)]
    came_a = lax.ppermute(fac_a, "xh", swap)
    send = pack((nx, ny, nz, nc), project(pair_state, token_pair_mask, input_weight), fac_b)
    swapped = lax.all_to_all(send, DEV, split_axis=0, concat_axis=0, tiled=True)
    terms = outer_terms(place, jnp.concatenate([fac_a, came_a], 1), outer_weight, rows)
    state = pair_state.reshape(points, width)
    gate = gates(state, input_weight)
    swapped, terms, gate = lax.optimization_barrier((swapped, terms, gate))
    partial, table = partials(swapped, half)
    back = lax.all_to_all(partial, ("xh",) + DEV, split_axis=0, concat_axis=0, tiled=True)

    flipped = lax.ppermute(table, "z", [(i, i ^ 1) for i in range(nz)])
    turns = [jnp.concatenate([table, flipped], 1)]
    for turn in range(1, ny):
        turns.append(lax.ppermute(turns[0], "y", [(i, (i + turn) % ny) for i in range(ny)]))
    turns += [lax.ppermute(value, "c", swap) for value in turns]
    opm = jnp.zeros((half, rows * width), jnp.float32)
    depth = turns[0].shape[1]
    for index, value in enumerate(turns):
        opm = opm + jnp.dot(
            value, terms[index * depth : (index + 1) * depth], preferred_element_type=jnp.float32
        )

    back = back.reshape(nr, devs, points).astype(jnp.float32)
    tri_sum = (back[0] + back[1]).astype(jnp.bfloat16).astype(jnp.float32)
    tri_norm = apply_layer_norm(tri_sum, 0).astype(jnp.bfloat16)
    tri_out = gate * jnp.einsum(
        "cp,cd->pd", tri_norm, output_weight, preferred_element_type=jnp.float32
    )
    opm = (opm * (1.0 / ALIGNMENT_ROWS)).reshape(half, rows, width)
    opm = jnp.transpose(opm, (1, 0, 2)).reshape(points, width)
    return (state.astype(jnp.float32) + opm + tri_out).astype(jnp.bfloat16).reshape(rows, half, width)


def solution(mesh):
    grid = Mesh(mesh.devices.reshape(2, 4, 8, 2, 2), ALL)
    inner = jax.shard_map(
        shards,
        mesh=grid,
        in_specs=(
            P(DEV, "xh", None),
            P(DEV, "xh"),
            P("xh", DEV, None),
            P("xh", DEV),
            P(),
            P(),
            P(),
            P(),
        ),
        out_specs=P(DEV, "xh", None),
        check_vma=False,
    )
    return inner
```

```python
import functools

import jax
import jax.numpy as jnp
from jax import lax
from jax.experimental import pallas as pl
from jax.experimental.pallas import tpu as pltpu
from jax.sharding import Mesh, PartitionSpec as P

FACTOR_WIDTH = 32
ALIGNMENT_ROWS = 128
VMEM_LIMIT = 56 * 1024 * 1024
SMALL_LIMIT = 16 * 1024 * 1024
DEV = ("xl", "y", "z", "c")
PLANE = ("xl", "y", "c", "xh")
ALL = ("xl", "y", "z", "c", "xh")


def apply_layer_norm(values, axis):
    center = jnp.mean(values, axis=axis, keepdims=True)
    spread = jnp.mean((values - center) ** 2, axis=axis, keepdims=True)
    return (values - center) * lax.rsqrt(spread + 1e-05)


def normalize(values):
    values = values - jnp.mean(values, axis=-1, keepdims=True)
    spread = jnp.mean(values * values, axis=-1, keepdims=True)
    return values * lax.rsqrt(spread + 1e-05)


def prepare_kernel(
    grid, state_ref, mask_ref, align_ref, align_mask_ref, weight_ref, align_weight_ref, send_ref, first_ref
):
    rows, half, width = state_ref.shape
    seqs, tokens, _ = align_ref.shape
    align = jnp.swapaxes(align_ref[...].astype(jnp.float32), 0, 1)
    columns = [normalize(align[tok]) for tok in range(tokens)]
    both = lax.dot_general(
        align_weight_ref[...],
        jnp.concatenate(columns, 0).astype(jnp.bfloat16),
        (((0,), (1,)), ((), ())),
        preferred_element_type=jnp.float32,
    )
    align_mask = align_mask_ref[...].astype(jnp.float32)
    tiles = []
    for tok in range(tokens):
        part = both[:, tok * seqs : (tok + 1) * seqs] * align_mask[tok : tok + 1, :]
        first_ref[:, tok * seqs : (tok + 1) * seqs] = part[:FACTOR_WIDTH].astype(jnp.bfloat16)
        part = part[FACTOR_WIDTH:]
        tiles.append(jnp.concatenate([part[: FACTOR_WIDTH // 2], part[FACTOR_WIDTH // 2 :]], 1))
    nx, ny, nz, nc = grid
    pieces = jnp.swapaxes(jnp.stack(tiles), 0, 1).reshape(ny, nx, 1, nc, tokens, 2 * seqs)
    pieces = jnp.broadcast_to(jnp.swapaxes(pieces, 0, 1), (nx, ny, nz, nc, tokens, 2 * seqs))
    send_ref[:, :, 2 * half :] = pieces.reshape(nx * ny * nz * nc, tokens, 2 * seqs).astype(jnp.bfloat16)

    weight = weight_ref[:, : 4 * width]
    factors = []
    for row in range(rows):
        normed = normalize(state_ref[row].astype(jnp.float32)).astype(jnp.bfloat16)
        stacked = lax.dot_general(
            weight, normed, (((0,), (1,)), ((), ())), preferred_element_type=jnp.float32
        )
        maskf = mask_ref[row : row + 1, :].astype(jnp.float32)
        sides = []
        for side in range(2):
            opened = stacked[2 * side * width : (2 * side + 1) * width]
            linear = stacked[(2 * side + 1) * width : (2 * side + 2) * width]
            sides.append(jax.nn.sigmoid(opened) * linear * maskf)
        factors.append(jnp.concatenate(sides, 1))
    send_ref[:, :, : 2 * half] = jnp.swapaxes(jnp.stack(factors), 0, 1).astype(jnp.bfloat16)


def prepare(grid, pair_state, mask, align, align_mask, weight, align_weight):
    rows, half, width = pair_state.shape
    seqs, tokens, _ = align.shape
    return pl.pallas_call(
        functools.partial(prepare_kernel, grid),
        out_shape=(
            jax.ShapeDtypeStruct((width, rows, 2 * half + 2 * seqs), jnp.bfloat16),
            jax.ShapeDtypeStruct((FACTOR_WIDTH, tokens * seqs), jnp.bfloat16),
        ),
        compiler_params=pltpu.CompilerParams(vmem_limit_bytes=VMEM_LIMIT),
        name="prepare",
    )(pair_state, mask, align, align_mask.T, weight, align_weight)


def gate_kernel(state_ref, weight_ref, out_ref):
    values = state_ref[...].astype(jnp.float32)
    values = values - jnp.mean(values, axis=-1, keepdims=True)
    spread = jnp.mean(values * values, axis=-1, keepdims=True)
    normed = (values * lax.rsqrt(spread + 1e-05)).astype(jnp.bfloat16)
    out_ref[...] = jax.nn.sigmoid(
        jnp.dot(normed, weight_ref[:, 4 * state_ref.shape[1] :], preferred_element_type=jnp.float32)
    )


def gates(state, weight):
    return pl.pallas_call(
        gate_kernel,
        out_shape=jax.ShapeDtypeStruct(state.shape, jnp.float32),
        name="gates",
    )(state, weight)


def terms_kernel(place_ref, first_ref, weight_ref, out_ref):
    cores, ny = 2, 4
    width = weight_ref.shape[1]
    rows = out_ref.shape[1] // width // cores
    columns = first_ref.shape[1] // 2 // cores
    seqs = columns // rows
    spread = first_ref[...]
    for turn in range(ny):
        for flip in range(2):
            piece = lax.rem(place_ref[0] + ny - turn, ny) * 2 + lax.rem(place_ref[3] + flip, 2)
            piece = piece * cores + place_ref[1]
            pair = [
                weight_ref[pl.ds((dh * FACTOR_WIDTH // 2 + piece) * FACTOR_WIDTH, FACTOR_WIDTH), :]
                for dh in range(2)
            ]
            product = lax.dot_general(
                spread, jnp.concatenate(pair, 1), (((0,), (0,)), ((), ())), preferred_element_type=jnp.float32
            ).astype(jnp.bfloat16)
            for core in range(cores):
                for other in range(2):
                    for row in range(rows):
                        start = (core * 2 + other) * columns + row * seqs
                        place = (core * rows + row) * width
                        for dh in range(2):
                            at = (((turn * 2 + other) * 2 + flip) * 2 + dh) * seqs
                            out_ref[at : at + seqs, place : place + width] = product[
                                start : start + seqs, dh * width : (dh + 1) * width
                            ]


def outer_terms(place, first, weight, rows):
    columns = first.shape[1]
    depth = FACTOR_WIDTH * columns // rows // 4
    width = weight.shape[1]
    return pl.pallas_call(
        terms_kernel,
        in_specs=[
            pl.BlockSpec(memory_space=pltpu.SMEM),
            pl.BlockSpec(memory_space=pltpu.VMEM),
            pl.BlockSpec(memory_space=pltpu.VMEM),
        ],
        out_shape=jax.ShapeDtypeStruct((depth, 2 * rows * width), jnp.bfloat16),
        cost_estimate=pl.CostEstimate(
            flops=4 * depth * rows * width * FACTOR_WIDTH, bytes_accessed=4 * depth * rows * width, transcendentals=0
        ),
        compiler_params=pltpu.CompilerParams(vmem_limit_bytes=VMEM_LIMIT),
        name="outer_terms",
    )(place, first, weight)


def outer_kernel(*refs):
    *turn_refs, terms_hbm, out_ref, terms_ref, sems = refs
    depth = turn_refs[0].shape[1]
    copies = []
    for index in range(len(turn_refs)):
        rows = pl.ds(index * depth, depth)
        copies.append(pltpu.make_async_copy(terms_hbm.at[rows], terms_ref.at[rows], sems.at[index]))
        copies[-1].start()
    total = 0.0
    for index, ref in enumerate(turn_refs):
        copies[index].wait()
        total = total + jnp.dot(
            ref[...], terms_ref[index * depth : (index + 1) * depth, :], preferred_element_type=jnp.float32
        )
    out_ref[...] = total


def outer_products(turns, terms):
    columns, depth = turns[0].shape
    width = terms.shape[1]
    vmem, hbm = pl.BlockSpec(memory_space=pltpu.VMEM), pl.BlockSpec(memory_space=pl.ANY)
    count = len(turns)
    return pl.pallas_call(
        outer_kernel,
        in_specs=[vmem] * count + [hbm],
        out_shape=jax.ShapeDtypeStruct((columns, width), jnp.float32),
        scratch_shapes=[pltpu.VMEM((count * depth, width), jnp.bfloat16), pltpu.SemaphoreType.DMA((count,))],
        cost_estimate=pl.CostEstimate(
            flops=2 * columns * depth * count * width,
            bytes_accessed=2 * depth * count * (width + columns) + 4 * columns * width,
            transcendentals=0,
        ),
        compiler_params=pltpu.CompilerParams(vmem_limit_bytes=SMALL_LIMIT),
        name="outer_products",
    )(*turns, terms)


def compact(values):
    groups, rows, lanes = values.shape
    pairs = values.reshape(groups // 2, 2, rows, lanes)
    return jnp.concatenate([pairs[:, 0], pairs[:, 1]], 1).reshape(groups * rows, lanes)


def partial_kernel(place_ref, swapped_ref, out_ref, own_ref, away_ref):
    devs, rows, lanes = swapped_ref.shape
    parts = 2
    half = out_ref.shape[2]
    values = compact(swapped_ref[...].astype(jnp.float32))
    left = values[:, :half].astype(jnp.bfloat16)
    right = values[:, half : 2 * half].astype(jnp.bfloat16)
    for part in range(parts):
        product = lax.dot_general(
            left,
            right[part * half : (part + 1) * half],
            (((1,), (1,)), ((), ())),
            preferred_element_type=jnp.float32,
        )
        product = product.reshape(devs // 2, 2 * rows, half)
        product = jnp.stack([product[:, :rows], product[:, rows:]], 1).reshape(devs, rows, half)
        out_ref[part * devs : (part + 1) * devs] = product.astype(jnp.bfloat16)
    table = values[:, 2 * half :].astype(jnp.bfloat16)
    mine = place_ref[2] == 0
    own_ref[...] = jnp.where(mine, table[:half], table[half:])
    away_ref[...] = jnp.where(mine, table[half:], table[:half])


def partials(place, swapped, half):
    devs, rows, lanes = swapped.shape
    table = jax.ShapeDtypeStruct((half, lanes - 2 * half), jnp.bfloat16)
    return pl.pallas_call(
        partial_kernel,
        in_specs=[pl.BlockSpec(memory_space=pltpu.SMEM), pl.BlockSpec(memory_space=pltpu.VMEM)],
        out_shape=(jax.ShapeDtypeStruct((2 * devs, rows, half), jnp.bfloat16), table, table),
        compiler_params=pltpu.CompilerParams(vmem_limit_bytes=SMALL_LIMIT),
        name="partials",
    )(place, swapped)


def merge_kernel(*refs):
    *part_refs, out_ref = refs
    depth = part_refs[0].shape[1]
    for index, ref in enumerate(part_refs):
        out_ref[:, index * depth : (index + 1) * depth] = ref[...]


def merge(*parts):
    columns, depth = parts[0].shape
    return pl.pallas_call(
        merge_kernel,
        out_shape=jax.ShapeDtypeStruct((columns, depth * len(parts)), jnp.bfloat16),
        compiler_params=pltpu.CompilerParams(vmem_limit_bytes=SMALL_LIMIT),
        name="merge",
    )(*parts)


def shards(
    pair_state,
    token_pair_mask,
    alignment_state,
    alignment_mask,
    input_weight,
    output_weight,
    alignment_weight,
    outer_weight,
):
    rows, half, width = pair_state.shape
    points = rows * half
    sizes = [lax.axis_size(name) for name in ALL]
    nx, ny, nz, nc, nr = sizes
    seqs = alignment_state.shape[0]
    devs = nx * ny * nz * nc
    place = jnp.stack([lax.axis_index(name) for name in ("y", "c", "xh", "xl")]).astype(jnp.int32)

    send, fac_a = prepare(
        (nx, ny, nz, nc), pair_state, token_pair_mask, alignment_state, alignment_mask, input_weight, alignment_weight
    )
    swap = [(0, 1), (1, 0)]
    came_a = lax.ppermute(fac_a, "xh", swap)
    swapped = lax.all_to_all(send, DEV, split_axis=0, concat_axis=0, tiled=True)
    both_a = jnp.concatenate([fac_a, came_a], 1)
    both_a = jnp.concatenate([both_a, lax.ppermute(both_a, "c", swap)], 1)
    terms = outer_terms(place, both_a, outer_weight, rows)
    state = pair_state.reshape(points, width)
    gate = gates(state, input_weight)
    swapped, terms, gate = lax.optimization_barrier((swapped, terms, gate))
    partial, own, away = partials(place, swapped, half)
    back = lax.all_to_all(partial, ("xh",) + DEV, split_axis=0, concat_axis=0, tiled=True)

    table = [
        own,
        lax.ppermute(own, "xl", swap),
        lax.ppermute(away, "xh", swap),
        lax.ppermute(away, ("xl", "xh"), [(0, 3), (1, 2), (2, 1), (3, 0)]),
    ]
    turns = [jnp.concatenate(table, 1)]
    for turn in range(1, ny):
        turns.append(lax.ppermute(turns[0], "y", [(i, (i + turn) % ny) for i in range(ny)]))
    depth = turns[0].shape[1]
    opm = outer_products(turns[:2], terms)
    for index in range(2, ny):
        opm = opm + jnp.dot(
            turns[index], terms[index * depth : (index + 1) * depth], preferred_element_type=jnp.float32
        )
    opm = opm * (1.0 / ALIGNMENT_ROWS)
    opm, other = opm[:, : rows * width], opm[:, rows * width :].astype(jnp.bfloat16)
    other, back = lax.optimization_barrier((other, back))
    other = lax.ppermute(other, "c", swap)

    back = back.reshape(nr, devs, points).astype(jnp.float32)
    tri_sum = (back[0] + back[1]).astype(jnp.bfloat16).astype(jnp.float32)
    tri_norm = apply_layer_norm(tri_sum, 0).astype(jnp.bfloat16)
    tri_out = gate * jnp.einsum(
        "cp,cd->pd", tri_norm, output_weight, preferred_element_type=jnp.float32
    )
    opm = (opm + other.astype(jnp.float32)).reshape(half, rows, width)
    opm = jnp.transpose(opm, (1, 0, 2)).reshape(points, width)
    return (state.astype(jnp.float32) + opm + tri_out).astype(jnp.bfloat16).reshape(rows, half, width)


def solution(mesh):
    grid = Mesh(mesh.devices.reshape(2, 4, 8, 2, 2), ALL)
    inner = jax.shard_map(
        shards,
        mesh=grid,
        in_specs=(
            P(DEV, "xh", None),
            P(DEV, "xh"),
            P("xh", DEV, None),
            P("xh", DEV),
            P(),
            P(),
            P(),
            P(),
        ),
        out_specs=P(DEV, "xh", None),
        check_vma=False,
    )
    return inner
```

```python
import functools

import jax
import jax.numpy as jnp
from jax import lax
from jax.experimental import pallas as pl
from jax.experimental.pallas import tpu as pltpu
from jax.sharding import Mesh, PartitionSpec as P

FACTOR_WIDTH = 32
ALIGNMENT_ROWS = 128
VMEM_LIMIT = 56 * 1024 * 1024
SMALL_LIMIT = 16 * 1024 * 1024
TURNS = (0, 2, 1, 3)
DEV = ("xl", "y", "z", "c")
PLANE = ("xl", "y", "c", "xh")
ALL = ("xl", "y", "z", "c", "xh")


def apply_layer_norm(values, axis):
    center = jnp.mean(values, axis=axis, keepdims=True)
    spread = jnp.mean((values - center) ** 2, axis=axis, keepdims=True)
    return (values - center) * lax.rsqrt(spread + 1e-05)


def normalize(values):
    values = values - jnp.mean(values, axis=-1, keepdims=True)
    spread = jnp.mean(values * values, axis=-1, keepdims=True)
    return values * lax.rsqrt(spread + 1e-05)


def prepare_kernel(
    grid, state_ref, mask_ref, align_ref, align_mask_ref, weight_ref, align_weight_ref, send_ref, first_ref
):
    rows, half, width = state_ref.shape
    seqs, tokens, _ = align_ref.shape
    align = jnp.swapaxes(align_ref[...].astype(jnp.float32), 0, 1)
    columns = [normalize(align[tok]) for tok in range(tokens)]
    both = lax.dot_general(
        align_weight_ref[...],
        jnp.concatenate(columns, 0).astype(jnp.bfloat16),
        (((0,), (1,)), ((), ())),
        preferred_element_type=jnp.float32,
    )
    align_mask = align_mask_ref[...].astype(jnp.float32)
    tiles = []
    for tok in range(tokens):
        part = both[:, tok * seqs : (tok + 1) * seqs] * align_mask[tok : tok + 1, :]
        first_ref[:, tok * seqs : (tok + 1) * seqs] = part[:FACTOR_WIDTH].astype(jnp.bfloat16)
        part = part[FACTOR_WIDTH:]
        tiles.append(jnp.concatenate([part[: FACTOR_WIDTH // 2], part[FACTOR_WIDTH // 2 :]], 1))
    nx, ny, nz, nc = grid
    pieces = jnp.swapaxes(jnp.stack(tiles), 0, 1).reshape(ny, nx, 1, nc, tokens, 2 * seqs)
    pieces = jnp.broadcast_to(jnp.swapaxes(pieces, 0, 1), (nx, ny, nz, nc, tokens, 2 * seqs))
    send_ref[:, :, 2 * half :] = pieces.reshape(nx * ny * nz * nc, tokens, 2 * seqs).astype(jnp.bfloat16)

    weight = weight_ref[:, : 4 * width]
    factors = []
    for row in range(rows):
        normed = normalize(state_ref[row].astype(jnp.float32)).astype(jnp.bfloat16)
        stacked = lax.dot_general(
            weight, normed, (((0,), (1,)), ((), ())), preferred_element_type=jnp.float32
        )
        maskf = mask_ref[row : row + 1, :].astype(jnp.float32)
        sides = []
        for side in range(2):
            opened = stacked[2 * side * width : (2 * side + 1) * width]
            linear = stacked[(2 * side + 1) * width : (2 * side + 2) * width]
            sides.append(jax.nn.sigmoid(opened) * linear * maskf)
        factors.append(jnp.concatenate(sides, 1))
    send_ref[:, :, : 2 * half] = jnp.swapaxes(jnp.stack(factors), 0, 1).astype(jnp.bfloat16)


def prepare(grid, pair_state, mask, align, align_mask, weight, align_weight):
    rows, half, width = pair_state.shape
    seqs, tokens, _ = align.shape
    return pl.pallas_call(
        functools.partial(prepare_kernel, grid),
        out_shape=(
            jax.ShapeDtypeStruct((width, rows, 2 * half + 2 * seqs), jnp.bfloat16),
            jax.ShapeDtypeStruct((FACTOR_WIDTH, tokens * seqs), jnp.bfloat16),
        ),
        compiler_params=pltpu.CompilerParams(vmem_limit_bytes=VMEM_LIMIT),
        name="prepare",
    )(pair_state, mask, align, align_mask.T, weight, align_weight)


def gate_kernel(state_ref, weight_ref, out_ref):
    values = state_ref[...].astype(jnp.float32)
    values = values - jnp.mean(values, axis=-1, keepdims=True)
    spread = jnp.mean(values * values, axis=-1, keepdims=True)
    normed = (values * lax.rsqrt(spread + 1e-05)).astype(jnp.bfloat16)
    out_ref[...] = jax.nn.sigmoid(
        jnp.dot(normed, weight_ref[:, 4 * state_ref.shape[1] :], preferred_element_type=jnp.float32)
    )


def gates(state, weight):
    return pl.pallas_call(
        gate_kernel,
        out_shape=jax.ShapeDtypeStruct(state.shape, jnp.float32),
        name="gates",
    )(state, weight)


def terms_kernel(place_ref, first_ref, came_ref, weight_ref, out_ref):
    cores, ny = 2, 4
    width = weight_ref.shape[1]
    rows = out_ref.shape[1] // width // cores
    columns = first_ref.shape[1] // cores
    seqs = columns // rows
    spread = []
    for core in range(cores):
        spread.append(first_ref[:, core * columns : (core + 1) * columns])
        for pair in range(columns // width):
            start = (core * columns // width + pair) * FACTOR_WIDTH
            spread.append(came_ref[start : start + FACTOR_WIDTH, :])
    spread = jnp.concatenate(spread, 1)
    for turn, shift in enumerate(TURNS):
        for flip in range(2):
            piece = lax.rem(place_ref[0] + ny - shift, ny) * 2 + lax.rem(place_ref[3] + flip, 2)
            piece = piece * cores + place_ref[1]
            pair = [
                weight_ref[pl.ds((dh * FACTOR_WIDTH // 2 + piece) * FACTOR_WIDTH, FACTOR_WIDTH), :]
                for dh in range(2)
            ]
            product = lax.dot_general(
                spread, jnp.concatenate(pair, 1), (((0,), (0,)), ((), ())), preferred_element_type=jnp.float32
            ).astype(jnp.bfloat16)
            for core in range(cores):
                for other in range(2):
                    for row in range(rows):
                        start = (core * 2 + other) * columns + row * seqs
                        place = (core * rows + row) * width
                        for dh in range(2):
                            at = (((flip * ny + turn) * 2 + other) * 2 + dh) * seqs
                            out_ref[at : at + seqs, place : place + width] = product[
                                start : start + seqs, dh * width : (dh + 1) * width
                            ]


def outer_terms(place, first, came, weight, rows):
    depth = FACTOR_WIDTH * first.shape[1] // rows // 2
    width = weight.shape[1]
    vmem = pl.BlockSpec(memory_space=pltpu.VMEM)
    return pl.pallas_call(
        terms_kernel,
        in_specs=[pl.BlockSpec(memory_space=pltpu.SMEM), vmem, vmem, vmem],
        out_shape=jax.ShapeDtypeStruct((depth, 2 * rows * width), jnp.bfloat16),
        cost_estimate=pl.CostEstimate(
            flops=4 * depth * rows * width * FACTOR_WIDTH, bytes_accessed=4 * depth * rows * width, transcendentals=0
        ),
        compiler_params=pltpu.CompilerParams(vmem_limit_bytes=SMALL_LIMIT),
        name="outer_terms",
    )(place, first, came, weight)


def outer_kernel(*refs):
    *turn_refs, terms_ref, out_ref = refs
    depth = turn_refs[0].shape[1]
    total = 0.0
    for index, ref in enumerate(turn_refs):
        total = total + jnp.dot(
            ref[...], terms_ref[index * depth : (index + 1) * depth, :], preferred_element_type=jnp.float32
        )
    out_ref[...] = total


def outer_products(turns, terms):
    columns, depth = turns[0].shape
    width = terms.shape[1]
    count = len(turns)
    return pl.pallas_call(
        outer_kernel,
        out_shape=jax.ShapeDtypeStruct((columns, width), jnp.float32),
        cost_estimate=pl.CostEstimate(
            flops=2 * columns * depth * count * width,
            bytes_accessed=2 * depth * count * (width + columns) + 4 * columns * width,
            transcendentals=0,
        ),
        compiler_params=pltpu.CompilerParams(vmem_limit_bytes=SMALL_LIMIT),
        name="outer_products",
    )(*turns, terms)


def compact(values):
    groups, rows, lanes = values.shape
    pairs = values.reshape(groups // 2, 2, rows, lanes)
    return jnp.concatenate([pairs[:, 0], pairs[:, 1]], 1).reshape(groups * rows, lanes)


def partial_kernel(flag_ref, swapped_ref, first_ref, out_ref, own_ref, away_ref):
    devs, rows, lanes = swapped_ref.shape
    parts = 2
    half = out_ref.shape[2]
    values = compact(swapped_ref[...].astype(jnp.float32))
    left = values[:, :half].astype(jnp.bfloat16)
    right = values[:, half : 2 * half].astype(jnp.bfloat16)
    for part in range(parts):
        product = lax.dot_general(
            left,
            right[part * half : (part + 1) * half],
            (((1,), (1,)), ((), ())),
            preferred_element_type=jnp.float32,
        )
        product = product.reshape(devs // 2, 2 * rows, half)
        product = jnp.stack([product[:, :rows], product[:, rows:]], 1).reshape(devs, rows, half)
        out_ref[part * devs : (part + 1) * devs] = product.astype(jnp.bfloat16)
    table = values[:, 2 * half :]
    mine = flag_ref[0:1, :] > 0.5
    own_ref[...] = jnp.where(mine, table[:half], table[half:]).astype(jnp.bfloat16)
    away_ref[:half] = jnp.where(mine, table[half:], table[:half]).astype(jnp.bfloat16)
    lanes = away_ref.shape[1]
    for index in range(first_ref.shape[1] // lanes):
        start = half + index * FACTOR_WIDTH
        away_ref[start : start + FACTOR_WIDTH] = first_ref[:, index * lanes : (index + 1) * lanes]


def partials(flag, swapped, first, half):
    devs, rows, lanes = swapped.shape
    lanes -= 2 * half
    return pl.pallas_call(
        partial_kernel,
        out_shape=(
            jax.ShapeDtypeStruct((2 * devs, rows, half), jnp.bfloat16),
            jax.ShapeDtypeStruct((half, lanes), jnp.bfloat16),
            jax.ShapeDtypeStruct((half + first.size // lanes, lanes), jnp.bfloat16),
        ),
        compiler_params=pltpu.CompilerParams(vmem_limit_bytes=SMALL_LIMIT),
        name="partials",
    )(flag, swapped, first)


def shards(
    pair_state,
    token_pair_mask,
    alignment_state,
    alignment_mask,
    input_weight,
    output_weight,
    alignment_weight,
    outer_weight,
):
    rows, half, width = pair_state.shape
    points = rows * half
    sizes = [lax.axis_size(name) for name in ALL]
    nx, ny, nz, nc, nr = sizes
    seqs = alignment_state.shape[0]
    devs = nx * ny * nz * nc
    place = jnp.stack([lax.axis_index(name) for name in ("y", "c", "xh", "xl")]).astype(jnp.int32)

    send, fac_a = prepare(
        (nx, ny, nz, nc), pair_state, token_pair_mask, alignment_state, alignment_mask, input_weight, alignment_weight
    )
    swap = [(0, 1), (1, 0)]
    both_a = jnp.concatenate([fac_a, lax.ppermute(fac_a, "c", swap)], 1)
    swapped = lax.all_to_all(send, DEV, split_axis=0, concat_axis=0, tiled=True)
    state = pair_state.reshape(points, width)
    gate = gates(state, input_weight)
    flag = jnp.broadcast_to(jnp.where(lax.axis_index("xh") == 0, 1.0, 0.0), (8, 2 * seqs)).astype(jnp.float32)
    swapped, both_a, gate, flag = lax.optimization_barrier((swapped, both_a, gate, flag))
    partial, own, away = partials(flag, swapped, both_a, half)
    back = lax.all_to_all(partial, ("xh",) + DEV, split_axis=0, concat_axis=0, tiled=True)

    came = lax.ppermute(away, "xh", swap)
    terms = outer_terms(place, both_a, came[half:], outer_weight, rows)
    turns = [lax.optimization_barrier(jnp.concatenate([own, came[:half]], 1))]
    for shift in TURNS[1:]:
        turns.append(lax.ppermute(turns[0], "y", [(i, (i + shift) % ny) for i in range(ny)]))
    turns += [lax.ppermute(value, "xl", swap) for value in turns]
    depth = turns[0].shape[1]
    opm = outer_products(turns[:7], terms)
    for index in range(7, len(turns)):
        opm = opm + jnp.dot(
            turns[index], terms[index * depth : (index + 1) * depth], preferred_element_type=jnp.float32
        )
    opm = opm * (1.0 / ALIGNMENT_ROWS)
    opm, other = opm[:, : rows * width], opm[:, rows * width :].astype(jnp.bfloat16)
    other, back = lax.optimization_barrier((other, back))
    other = lax.ppermute(other, "c", swap)

    back = back.reshape(nr, devs, points).astype(jnp.float32)
    tri_sum = (back[0] + back[1]).astype(jnp.bfloat16).astype(jnp.float32)
    tri_norm = apply_layer_norm(tri_sum, 0).astype(jnp.bfloat16)
    tri_out = gate * jnp.einsum(
        "cp,cd->pd", tri_norm, output_weight, preferred_element_type=jnp.float32
    )
    opm = (opm + other.astype(jnp.float32)).reshape(half, rows, width)
    opm = jnp.transpose(opm, (1, 0, 2)).reshape(points, width)
    return (state.astype(jnp.float32) + opm + tri_out).astype(jnp.bfloat16).reshape(rows, half, width)


def solution(mesh):
    grid = Mesh(mesh.devices.reshape(2, 4, 8, 2, 2), ALL)
    inner = jax.shard_map(
        shards,
        mesh=grid,
        in_specs=(
            P(DEV, "xh", None),
            P(DEV, "xh"),
            P("xh", DEV, None),
            P("xh", DEV),
            P(),
            P(),
            P(),
            P(),
        ),
        out_specs=P(DEV, "xh", None),
        check_vma=False,
    )
    return inner
```

```python
import functools

import jax
import jax.numpy as jnp
from jax import lax
from jax.experimental import pallas as pl
from jax.experimental.pallas import tpu as pltpu
from jax.sharding import Mesh, PartitionSpec as P

FACTOR_WIDTH = 32
ALIGNMENT_ROWS = 128
VMEM_LIMIT = 56 * 1024 * 1024
SMALL_LIMIT = 16 * 1024 * 1024
TURNS = (0, 2, 1, 3)
DEV = ("xl", "y", "z", "c")
PLANE = ("xl", "y", "c", "xh")
ALL = ("xl", "y", "z", "c", "xh")


def apply_layer_norm(values, axis):
    center = jnp.mean(values, axis=axis, keepdims=True)
    spread = jnp.mean((values - center) ** 2, axis=axis, keepdims=True)
    return (values - center) * lax.rsqrt(spread + 1e-05)


def normalize(values):
    values = values - jnp.mean(values, axis=-1, keepdims=True)
    spread = jnp.mean(values * values, axis=-1, keepdims=True)
    return values * lax.rsqrt(spread + 1e-05)


def prepare_kernel(
    grid, state_ref, mask_ref, align_ref, align_mask_ref, weight_ref, align_weight_ref, send_ref, first_ref
):
    rows, half, width = state_ref.shape
    seqs, tokens, _ = align_ref.shape
    align = jnp.swapaxes(align_ref[...].astype(jnp.float32), 0, 1)
    columns = [normalize(align[tok]) for tok in range(tokens)]
    both = lax.dot_general(
        align_weight_ref[...],
        jnp.concatenate(columns, 0).astype(jnp.bfloat16),
        (((0,), (1,)), ((), ())),
        preferred_element_type=jnp.float32,
    )
    align_mask = align_mask_ref[...].astype(jnp.float32)
    tiles = []
    for tok in range(tokens):
        part = both[:, tok * seqs : (tok + 1) * seqs] * align_mask[tok : tok + 1, :]
        first_ref[:, tok * seqs : (tok + 1) * seqs] = part[:FACTOR_WIDTH].astype(jnp.bfloat16)
        part = part[FACTOR_WIDTH:]
        tiles.append(jnp.concatenate([part[: FACTOR_WIDTH // 2], part[FACTOR_WIDTH // 2 :]], 1))
    nx, ny, nz, nc = grid
    pieces = jnp.swapaxes(jnp.stack(tiles), 0, 1).reshape(ny, nx, 1, nc, tokens, 2 * seqs)
    pieces = jnp.broadcast_to(jnp.swapaxes(pieces, 0, 1), (nx, ny, nz, nc, tokens, 2 * seqs))
    send_ref[:, :, 2 * half :] = pieces.reshape(nx * ny * nz * nc, tokens, 2 * seqs).astype(jnp.bfloat16)

    weight = weight_ref[:, : 4 * width]
    factors = []
    for row in range(rows):
        normed = normalize(state_ref[row].astype(jnp.float32)).astype(jnp.bfloat16)
        stacked = lax.dot_general(
            weight, normed, (((0,), (1,)), ((), ())), preferred_element_type=jnp.float32
        )
        maskf = mask_ref[row : row + 1, :].astype(jnp.float32)
        sides = []
        for side in range(2):
            opened = stacked[2 * side * width : (2 * side + 1) * width]
            linear = stacked[(2 * side + 1) * width : (2 * side + 2) * width]
            sides.append(jax.nn.sigmoid(opened) * linear * maskf)
        factors.append(jnp.concatenate(sides, 1))
    send_ref[:, :, : 2 * half] = jnp.swapaxes(jnp.stack(factors), 0, 1).astype(jnp.bfloat16)


def prepare(grid, pair_state, mask, align, align_mask, weight, align_weight):
    rows, half, width = pair_state.shape
    seqs, tokens, _ = align.shape
    return pl.pallas_call(
        functools.partial(prepare_kernel, grid),
        out_shape=(
            jax.ShapeDtypeStruct((width, rows, 2 * half + 2 * seqs), jnp.bfloat16),
            jax.ShapeDtypeStruct((FACTOR_WIDTH, tokens * seqs), jnp.bfloat16),
        ),
        compiler_params=pltpu.CompilerParams(vmem_limit_bytes=VMEM_LIMIT),
        name="prepare",
    )(pair_state, mask, align, align_mask.T, weight, align_weight)


def gate_kernel(state_ref, weight_ref, out_ref):
    values = state_ref[...].astype(jnp.float32)
    values = values - jnp.mean(values, axis=-1, keepdims=True)
    spread = jnp.mean(values * values, axis=-1, keepdims=True)
    normed = (values * lax.rsqrt(spread + 1e-05)).astype(jnp.bfloat16)
    out_ref[...] = jax.nn.sigmoid(
        jnp.dot(normed, weight_ref[:, 4 * state_ref.shape[1] :], preferred_element_type=jnp.float32)
    )


def gates(state, weight):
    return pl.pallas_call(
        gate_kernel,
        out_shape=jax.ShapeDtypeStruct(state.shape, jnp.float32),
        name="gates",
    )(state, weight)


def terms_kernel(place_ref, first_ref, came_ref, weight_ref, out_ref):
    cores, ny = 2, 4
    width = weight_ref.shape[1]
    rows = out_ref.shape[1] // width // cores
    columns = first_ref.shape[1] // cores
    seqs = columns // rows
    spread = []
    for core in range(cores):
        spread.append(first_ref[:, core * columns : (core + 1) * columns])
        for pair in range(columns // width):
            start = (core * columns // width + pair) * FACTOR_WIDTH
            spread.append(came_ref[start : start + FACTOR_WIDTH, :])
    spread = jnp.concatenate(spread, 1)
    for turn, shift in enumerate(TURNS):
        for flip in range(2):
            piece = lax.rem(place_ref[0] + ny - shift, ny) * 2 + lax.rem(place_ref[3] + flip, 2)
            piece = piece * cores + place_ref[1]
            pair = [
                weight_ref[pl.ds((dh * FACTOR_WIDTH // 2 + piece) * FACTOR_WIDTH, FACTOR_WIDTH), :]
                for dh in range(2)
            ]
            product = lax.dot_general(
                spread, jnp.concatenate(pair, 1), (((0,), (0,)), ((), ())), preferred_element_type=jnp.float32
            ).astype(jnp.bfloat16)
            for core in range(cores):
                for other in range(2):
                    for row in range(rows):
                        start = (core * 2 + other) * columns + row * seqs
                        place = (core * rows + row) * width
                        for dh in range(2):
                            at = (((flip * ny + turn) * 2 + other) * 2 + dh) * seqs
                            out_ref[at : at + seqs, place : place + width] = product[
                                start : start + seqs, dh * width : (dh + 1) * width
                            ]


def outer_terms(place, first, came, weight, rows):
    depth = FACTOR_WIDTH * first.shape[1] // rows // 2
    width = weight.shape[1]
    vmem = pl.BlockSpec(memory_space=pltpu.VMEM)
    return pl.pallas_call(
        terms_kernel,
        in_specs=[pl.BlockSpec(memory_space=pltpu.SMEM), vmem, vmem, vmem],
        out_shape=jax.ShapeDtypeStruct((depth, 2 * rows * width), jnp.bfloat16),
        cost_estimate=pl.CostEstimate(
            flops=4 * depth * rows * width * FACTOR_WIDTH, bytes_accessed=4 * depth * rows * width, transcendentals=0
        ),
        compiler_params=pltpu.CompilerParams(vmem_limit_bytes=SMALL_LIMIT),
        name="outer_terms",
    )(place, first, came, weight)


def early_kernel(*refs):
    *turn_refs, terms_ref, out_ref = refs
    depth = turn_refs[0].shape[1]
    total = 0.0
    for index, ref in enumerate(turn_refs):
        total = total + jnp.dot(
            ref[...], terms_ref[index * depth : (index + 1) * depth, :], preferred_element_type=jnp.float32
        )
    out_ref[...] = total


def early_products(turns, terms):
    columns, depth = turns[0].shape
    width = terms.shape[1]
    count = len(turns)
    return pl.pallas_call(
        early_kernel,
        out_shape=jax.ShapeDtypeStruct((columns, width), jnp.float32),
        cost_estimate=pl.CostEstimate(
            flops=2 * columns * depth * count * width,
            bytes_accessed=2 * depth * count * (width + columns) + 4 * columns * width,
            transcendentals=0,
        ),
        compiler_params=pltpu.CompilerParams(vmem_limit_bytes=SMALL_LIMIT),
        name="early_products",
    )(*turns, terms)


def late_kernel(offset, *refs):
    *turn_refs, total_ref, terms_ref, own_ref, other_ref = refs
    depth = turn_refs[0].shape[1]
    rows, _, width = own_ref.shape
    total = total_ref[...]
    for index, ref in enumerate(turn_refs):
        start = offset + index * depth
        total = total + jnp.dot(ref[...], terms_ref[start : start + depth, :], preferred_element_type=jnp.float32)
    total = total * (1.0 / ALIGNMENT_ROWS)
    for row in range(rows):
        own_ref[row] = total[:, row * width : (row + 1) * width]
        other_ref[row] = total[:, (rows + row) * width : (rows + row + 1) * width].astype(jnp.bfloat16)


def late_products(turns, total, terms, rows):
    columns, depth = turns[0].shape
    width = terms.shape[1]
    shape = (rows, columns, width // 2 // rows)
    count = len(turns)
    return pl.pallas_call(
        functools.partial(late_kernel, terms.shape[0] - count * depth),
        out_shape=(
            jax.ShapeDtypeStruct(shape, jnp.float32),
            jax.ShapeDtypeStruct(shape, jnp.bfloat16),
        ),
        cost_estimate=pl.CostEstimate(
            flops=2 * columns * depth * count * width,
            bytes_accessed=2 * depth * count * (width + columns) + 7 * columns * width,
            transcendentals=0,
        ),
        compiler_params=pltpu.CompilerParams(vmem_limit_bytes=SMALL_LIMIT),
        name="late_products",
    )(*turns, total, terms)


def compact(values):
    groups, rows, lanes = values.shape
    pairs = values.reshape(groups // 2, 2, rows, lanes)
    return jnp.concatenate([pairs[:, 0], pairs[:, 1]], 1).reshape(groups * rows, lanes)


def partial_kernel(flag_ref, swapped_ref, first_ref, out_ref, own_ref, away_ref):
    devs, rows, lanes = swapped_ref.shape
    parts = 2
    half = out_ref.shape[2]
    values = compact(swapped_ref[...].astype(jnp.float32))
    left = values[:, :half].astype(jnp.bfloat16)
    right = values[:, half : 2 * half].astype(jnp.bfloat16)
    for part in range(parts):
        product = lax.dot_general(
            left,
            right[part * half : (part + 1) * half],
            (((1,), (1,)), ((), ())),
            preferred_element_type=jnp.float32,
        )
        product = product.reshape(devs // 2, 2 * rows, half)
        product = jnp.stack([product[:, :rows], product[:, rows:]], 1).reshape(devs, rows, half)
        out_ref[part * devs : (part + 1) * devs] = product.astype(jnp.bfloat16)
    table = values[:, 2 * half :]
    mine = flag_ref[0:1, :] > 0.5
    own_ref[...] = jnp.where(mine, table[:half], table[half:]).astype(jnp.bfloat16)
    away_ref[:half] = jnp.where(mine, table[half:], table[:half]).astype(jnp.bfloat16)
    lanes = away_ref.shape[1]
    for index in range(first_ref.shape[1] // lanes):
        start = half + index * FACTOR_WIDTH
        away_ref[start : start + FACTOR_WIDTH] = first_ref[:, index * lanes : (index + 1) * lanes]


def partials(flag, swapped, first, half):
    devs, rows, lanes = swapped.shape
    lanes -= 2 * half
    return pl.pallas_call(
        partial_kernel,
        out_shape=(
            jax.ShapeDtypeStruct((2 * devs, rows, half), jnp.bfloat16),
            jax.ShapeDtypeStruct((half, lanes), jnp.bfloat16),
            jax.ShapeDtypeStruct((half + first.size // lanes, lanes), jnp.bfloat16),
        ),
        compiler_params=pltpu.CompilerParams(vmem_limit_bytes=SMALL_LIMIT),
        name="partials",
    )(flag, swapped, first)


def shards(
    pair_state,
    token_pair_mask,
    alignment_state,
    alignment_mask,
    input_weight,
    output_weight,
    alignment_weight,
    outer_weight,
):
    rows, half, width = pair_state.shape
    points = rows * half
    sizes = [lax.axis_size(name) for name in ALL]
    nx, ny, nz, nc, nr = sizes
    seqs = alignment_state.shape[0]
    devs = nx * ny * nz * nc
    place = jnp.stack([lax.axis_index(name) for name in ("y", "c", "xh", "xl")]).astype(jnp.int32)

    send, fac_a = prepare(
        (nx, ny, nz, nc), pair_state, token_pair_mask, alignment_state, alignment_mask, input_weight, alignment_weight
    )
    swap = [(0, 1), (1, 0)]
    both_a = jnp.concatenate([fac_a, lax.ppermute(fac_a, "c", swap)], 1)
    swapped = lax.all_to_all(send, DEV, split_axis=0, concat_axis=0, tiled=True)
    state = pair_state.reshape(points, width)
    gate = gates(state, input_weight)
    flag = jnp.broadcast_to(jnp.where(lax.axis_index("xh") == 0, 1.0, 0.0), (8, 2 * seqs)).astype(jnp.float32)
    swapped, both_a, gate, flag = lax.optimization_barrier((swapped, both_a, gate, flag))
    partial, own, away = partials(flag, swapped, both_a, half)
    back = lax.all_to_all(partial, ("xh",) + DEV, split_axis=0, concat_axis=0, tiled=True)

    came = lax.ppermute(away, "xh", swap)
    terms = outer_terms(place, both_a, came[half:], outer_weight, rows)
    turns = [lax.optimization_barrier(jnp.concatenate([own, came[:half]], 1))]
    for shift in TURNS[1:]:
        turns.append(lax.ppermute(turns[0], "y", [(i, (i + shift) % ny) for i in range(ny)]))
    turns += [lax.ppermute(value, "xl", swap) for value in turns]
    depth = turns[0].shape[1]
    opm = early_products(turns[:5], terms)
    for index in range(5, 7):
        opm = opm + jnp.dot(
            turns[index], terms[index * depth : (index + 1) * depth], preferred_element_type=jnp.float32
        )
    opm, other = late_products(turns[7:], opm, terms, rows)
    other, back = lax.optimization_barrier((other, back))
    other = lax.ppermute(other, "c", swap)

    back = back.reshape(nr, devs, points).astype(jnp.float32)
    tri_sum = (back[0] + back[1]).astype(jnp.bfloat16).astype(jnp.float32)
    tri_norm = apply_layer_norm(tri_sum, 0).astype(jnp.bfloat16)
    tri_out = gate * jnp.einsum(
        "cp,cd->pd", tri_norm, output_weight, preferred_element_type=jnp.float32
    )
    base = lax.optimization_barrier(state.astype(jnp.float32) + tri_out + opm.reshape(points, width))
    return (base + other.reshape(points, width).astype(jnp.float32)).astype(jnp.bfloat16).reshape(rows, half, width)


def solution(mesh):
    grid = Mesh(mesh.devices.reshape(2, 4, 8, 2, 2), ALL)
    inner = jax.shard_map(
        shards,
        mesh=grid,
        in_specs=(
            P(DEV, "xh", None),
            P(DEV, "xh"),
            P("xh", DEV, None),
            P("xh", DEV),
            P(),
            P(),
            P(),
            P(),
        ),
        out_specs=P(DEV, "xh", None),
        check_vma=False,
    )
    return inner
```

```python
import functools

import jax
import jax.numpy as jnp
from jax import lax
from jax.experimental import pallas as pl
from jax.experimental.pallas import tpu as pltpu
from jax.sharding import Mesh, PartitionSpec as P

FACTOR_WIDTH = 32
ALIGNMENT_ROWS = 128
VMEM_LIMIT = 56 * 1024 * 1024
SMALL_LIMIT = 16 * 1024 * 1024
TURNS = (0, 2, 1, 3)
DEV = ("xl", "y", "z", "c")
PLANE = ("xl", "y", "c", "xh")
ALL = ("xl", "y", "z", "c", "xh")


def apply_layer_norm(values, axis):
    center = jnp.mean(values, axis=axis, keepdims=True)
    spread = jnp.mean((values - center) ** 2, axis=axis, keepdims=True)
    return (values - center) * lax.rsqrt(spread + 1e-05)


def normalize(values):
    values = values - jnp.mean(values, axis=-1, keepdims=True)
    spread = jnp.mean(values * values, axis=-1, keepdims=True)
    return values * lax.rsqrt(spread + 1e-05)


def prepare_kernel(
    grid, state_ref, mask_ref, align_ref, align_mask_ref, weight_ref, align_weight_ref, send_ref, first_ref
):
    rows, half, width = state_ref.shape
    seqs, tokens, _ = align_ref.shape
    align = jnp.swapaxes(align_ref[...].astype(jnp.float32), 0, 1)
    columns = [normalize(align[tok]) for tok in range(tokens)]
    both = lax.dot_general(
        align_weight_ref[...],
        jnp.concatenate(columns, 0).astype(jnp.bfloat16),
        (((0,), (1,)), ((), ())),
        preferred_element_type=jnp.float32,
    )
    align_mask = align_mask_ref[...].astype(jnp.float32)
    tiles = []
    for tok in range(tokens):
        part = both[:, tok * seqs : (tok + 1) * seqs] * align_mask[tok : tok + 1, :]
        first_ref[:, tok * seqs : (tok + 1) * seqs] = part[:FACTOR_WIDTH].astype(jnp.bfloat16)
        part = part[FACTOR_WIDTH:]
        tiles.append(jnp.concatenate([part[: FACTOR_WIDTH // 2], part[FACTOR_WIDTH // 2 :]], 1))
    nx, ny, nz, nc = grid
    pieces = jnp.swapaxes(jnp.stack(tiles), 0, 1).reshape(ny, nx, 1, nc, tokens, 2 * seqs)
    pieces = jnp.broadcast_to(jnp.swapaxes(pieces, 0, 1), (nx, ny, nz, nc, tokens, 2 * seqs))
    send_ref[:, :, 2 * half :] = pieces.reshape(nx * ny * nz * nc, tokens, 2 * seqs).astype(jnp.bfloat16)

    weight = weight_ref[:, : 4 * width]
    factors = []
    for row in range(rows):
        normed = normalize(state_ref[row].astype(jnp.float32)).astype(jnp.bfloat16)
        stacked = lax.dot_general(
            weight, normed, (((0,), (1,)), ((), ())), preferred_element_type=jnp.float32
        )
        maskf = mask_ref[row : row + 1, :].astype(jnp.float32)
        sides = []
        for side in range(2):
            opened = stacked[2 * side * width : (2 * side + 1) * width]
            linear = stacked[(2 * side + 1) * width : (2 * side + 2) * width]
            sides.append(jax.nn.sigmoid(opened) * linear * maskf)
        factors.append(jnp.concatenate(sides, 1))
    send_ref[:, :, : 2 * half] = jnp.swapaxes(jnp.stack(factors), 0, 1).astype(jnp.bfloat16)


def prepare(grid, pair_state, mask, align, align_mask, weight, align_weight):
    rows, half, width = pair_state.shape
    seqs, tokens, _ = align.shape
    return pl.pallas_call(
        functools.partial(prepare_kernel, grid),
        out_shape=(
            jax.ShapeDtypeStruct((width, rows, 2 * half + 2 * seqs), jnp.bfloat16),
            jax.ShapeDtypeStruct((FACTOR_WIDTH, tokens * seqs), jnp.bfloat16),
        ),
        compiler_params=pltpu.CompilerParams(vmem_limit_bytes=VMEM_LIMIT),
        name="prepare",
    )(pair_state, mask, align, align_mask.T, weight, align_weight)


def gate_kernel(state_ref, weight_ref, out_ref):
    values = state_ref[...].astype(jnp.float32)
    values = values - jnp.mean(values, axis=-1, keepdims=True)
    spread = jnp.mean(values * values, axis=-1, keepdims=True)
    normed = (values * lax.rsqrt(spread + 1e-05)).astype(jnp.bfloat16)
    out_ref[...] = jax.nn.sigmoid(
        jnp.dot(normed, weight_ref[:, 4 * state_ref.shape[1] :], preferred_element_type=jnp.float32)
    )


def gates(state, weight):
    return pl.pallas_call(
        gate_kernel,
        out_shape=jax.ShapeDtypeStruct(state.shape, jnp.float32),
        name="gates",
    )(state, weight)


def terms_kernel(place_ref, first_ref, came_ref, weight_ref, out_ref):
    cores, ny = 2, 4
    width = weight_ref.shape[1]
    rows = out_ref.shape[1] // width // cores
    columns = first_ref.shape[1] // cores
    seqs = columns // rows
    spread = []
    for core in range(cores):
        spread.append(first_ref[:, core * columns : (core + 1) * columns])
        for pair in range(columns // width):
            start = (core * columns // width + pair) * FACTOR_WIDTH
            spread.append(came_ref[start : start + FACTOR_WIDTH, :])
    spread = jnp.concatenate(spread, 1)
    for turn, shift in enumerate(TURNS):
        for flip in range(2):
            piece = lax.rem(place_ref[0] + ny - shift, ny) * 2 + lax.rem(place_ref[3] + flip, 2)
            piece = piece * cores + place_ref[1]
            pair = [
                weight_ref[pl.ds((dh * FACTOR_WIDTH // 2 + piece) * FACTOR_WIDTH, FACTOR_WIDTH), :]
                for dh in range(2)
            ]
            product = lax.dot_general(
                spread, jnp.concatenate(pair, 1), (((0,), (0,)), ((), ())), preferred_element_type=jnp.float32
            ).astype(jnp.bfloat16)
            for core in range(cores):
                for other in range(2):
                    for row in range(rows):
                        start = (core * 2 + other) * columns + row * seqs
                        place = (core * rows + row) * width
                        for dh in range(2):
                            at = (((flip * ny + turn) * 2 + other) * 2 + dh) * seqs
                            out_ref[at : at + seqs, place : place + width] = product[
                                start : start + seqs, dh * width : (dh + 1) * width
                            ]


def outer_terms(place, first, came, weight, rows):
    depth = FACTOR_WIDTH * first.shape[1] // rows // 2
    width = weight.shape[1]
    vmem = pl.BlockSpec(memory_space=pltpu.VMEM)
    return pl.pallas_call(
        terms_kernel,
        in_specs=[pl.BlockSpec(memory_space=pltpu.SMEM), vmem, vmem, vmem],
        out_shape=jax.ShapeDtypeStruct((depth, 2 * rows * width), jnp.bfloat16),
        cost_estimate=pl.CostEstimate(
            flops=4 * depth * rows * width * FACTOR_WIDTH, bytes_accessed=4 * depth * rows * width, transcendentals=0
        ),
        compiler_params=pltpu.CompilerParams(vmem_limit_bytes=SMALL_LIMIT),
        name="outer_terms",
    )(place, first, came, weight)


def early_kernel(*refs):
    *turn_refs, terms_ref, out_ref = refs
    depth = turn_refs[0].shape[1]
    total = 0.0
    for index, ref in enumerate(turn_refs):
        total = total + jnp.dot(
            ref[...], terms_ref[index * depth : (index + 1) * depth, :], preferred_element_type=jnp.float32
        )
    out_ref[...] = total


def early_products(turns, terms):
    columns, depth = turns[0].shape
    width = terms.shape[1]
    count = len(turns)
    return pl.pallas_call(
        early_kernel,
        out_shape=jax.ShapeDtypeStruct((columns, width), jnp.float32),
        cost_estimate=pl.CostEstimate(
            flops=2 * columns * depth * count * width,
            bytes_accessed=2 * depth * count * (width + columns) + 4 * columns * width,
            transcendentals=0,
        ),
        compiler_params=pltpu.CompilerParams(vmem_limit_bytes=SMALL_LIMIT),
        name="early_products",
    )(*turns, terms)


def late_kernel(offset, *refs):
    *turn_refs, total_ref, terms_ref, own_ref, other_ref = refs
    depth = turn_refs[0].shape[1]
    rows, _, width = own_ref.shape
    total = total_ref[...]
    for index, ref in enumerate(turn_refs):
        start = offset + index * depth
        total = total + jnp.dot(ref[...], terms_ref[start : start + depth, :], preferred_element_type=jnp.float32)
    total = total * (1.0 / ALIGNMENT_ROWS)
    for row in range(rows):
        own_ref[row] = total[:, row * width : (row + 1) * width]
        other_ref[row] = total[:, (rows + row) * width : (rows + row + 1) * width].astype(jnp.bfloat16)


def late_products(turns, total, terms, rows):
    columns, depth = turns[0].shape
    width = terms.shape[1]
    shape = (rows, columns, width // 2 // rows)
    count = len(turns)
    return pl.pallas_call(
        functools.partial(late_kernel, terms.shape[0] - count * depth),
        out_shape=(
            jax.ShapeDtypeStruct(shape, jnp.float32),
            jax.ShapeDtypeStruct(shape, jnp.bfloat16),
        ),
        cost_estimate=pl.CostEstimate(
            flops=2 * columns * depth * count * width,
            bytes_accessed=2 * depth * count * (width + columns) + 7 * columns * width,
            transcendentals=0,
        ),
        compiler_params=pltpu.CompilerParams(vmem_limit_bytes=SMALL_LIMIT),
        name="late_products",
    )(*turns, total, terms)


def compact(values):
    groups, rows, lanes = values.shape
    pairs = values.reshape(groups // 2, 2, rows, lanes)
    return jnp.concatenate([pairs[:, 0], pairs[:, 1]], 1).reshape(groups * rows, lanes)


def partial_kernel(flag_ref, swapped_ref, first_ref, out_ref, own_ref, away_ref):
    devs, rows, lanes = swapped_ref.shape
    parts = 2
    half = out_ref.shape[2]
    values = compact(swapped_ref[...].astype(jnp.float32))
    left = values[:, :half].astype(jnp.bfloat16)
    right = values[:, half : 2 * half].astype(jnp.bfloat16)
    for part in range(parts):
        product = lax.dot_general(
            left,
            right[part * half : (part + 1) * half],
            (((1,), (1,)), ((), ())),
            preferred_element_type=jnp.float32,
        )
        product = product.reshape(devs // 2, 2 * rows, half)
        product = jnp.stack([product[:, :rows], product[:, rows:]], 1).reshape(devs, rows, half)
        out_ref[part * devs : (part + 1) * devs] = product.astype(jnp.bfloat16)
    table = values[:, 2 * half :]
    mine = flag_ref[0:1, :] > 0.5
    own_ref[...] = jnp.where(mine, table[:half], table[half:]).astype(jnp.bfloat16)
    away_ref[:half] = jnp.where(mine, table[half:], table[:half]).astype(jnp.bfloat16)
    lanes = away_ref.shape[1]
    for index in range(first_ref.shape[1] // lanes):
        start = half + index * FACTOR_WIDTH
        away_ref[start : start + FACTOR_WIDTH] = first_ref[:, index * lanes : (index + 1) * lanes]


def partials(flag, swapped, first, half):
    devs, rows, lanes = swapped.shape
    lanes -= 2 * half
    return pl.pallas_call(
        partial_kernel,
        out_shape=(
            jax.ShapeDtypeStruct((2 * devs, rows, half), jnp.bfloat16),
            jax.ShapeDtypeStruct((half, lanes), jnp.bfloat16),
            jax.ShapeDtypeStruct((half + first.size // lanes, lanes), jnp.bfloat16),
        ),
        compiler_params=pltpu.CompilerParams(vmem_limit_bytes=SMALL_LIMIT),
        name="partials",
    )(flag, swapped, first)


def shards(
    pair_state,
    token_pair_mask,
    alignment_state,
    alignment_mask,
    input_weight,
    output_weight,
    alignment_weight,
    outer_weight,
):
    rows, half, width = pair_state.shape
    points = rows * half
    sizes = [lax.axis_size(name) for name in ALL]
    nx, ny, nz, nc, nr = sizes
    seqs = alignment_state.shape[0]
    devs = nx * ny * nz * nc
    place = jnp.stack([lax.axis_index(name) for name in ("y", "c", "xh", "xl")]).astype(jnp.int32)

    send, fac_a = prepare(
        (nx, ny, nz, nc), pair_state, token_pair_mask, alignment_state, alignment_mask, input_weight, alignment_weight
    )
    swap = [(0, 1), (1, 0)]
    both_a = jnp.concatenate([fac_a, lax.ppermute(fac_a, "c", swap)], 1)
    swapped = lax.all_to_all(send, DEV, split_axis=0, concat_axis=0, tiled=True)
    state = pair_state.reshape(points, width)
    gate = gates(state, input_weight)
    flag = jnp.broadcast_to(jnp.where(lax.axis_index("xh") == 0, 1.0, 0.0), (8, 2 * seqs)).astype(jnp.float32)
    swapped, both_a, gate, flag = lax.optimization_barrier((swapped, both_a, gate, flag))
    partial, own, away = partials(flag, swapped, both_a, half)
    back = lax.all_to_all(partial, ("xh",) + DEV, split_axis=0, concat_axis=0, tiled=True)

    came = lax.ppermute(away, "xh", swap)
    terms = outer_terms(place, both_a, came[half:], outer_weight, rows)
    turns = [lax.optimization_barrier(jnp.concatenate([own, came[:half]], 1))]
    for shift in TURNS[1:]:
        turns.append(lax.ppermute(turns[0], "y", [(i, (i + shift) % ny) for i in range(ny)]))
    turns += [lax.ppermute(value, "xl", swap) for value in turns]
    depth = turns[0].shape[1]
    opm = early_products(turns[:5], terms)
    for index in range(5, 7):
        opm = opm + jnp.dot(
            turns[index], terms[index * depth : (index + 1) * depth], preferred_element_type=jnp.float32
        )
    opm, other = late_products(turns[7:], opm, terms, rows)
    other = lax.ppermute(other, "c", swap)

    back = back.reshape(nr, devs, points).astype(jnp.float32)
    tri_sum = (back[0] + back[1]).astype(jnp.bfloat16).astype(jnp.float32)
    tri_norm = apply_layer_norm(tri_sum, 0).astype(jnp.bfloat16)
    tri_out = gate * jnp.einsum(
        "cp,cd->pd", tri_norm, output_weight, preferred_element_type=jnp.float32
    )
    base = lax.optimization_barrier(state.astype(jnp.float32) + tri_out + opm.reshape(points, width))
    return (base + other.reshape(points, width).astype(jnp.float32)).astype(jnp.bfloat16).reshape(rows, half, width)


def solution(mesh):
    grid = Mesh(mesh.devices.reshape(2, 4, 8, 2, 2), ALL)
    inner = jax.shard_map(
        shards,
        mesh=grid,
        in_specs=(
            P(DEV, "xh", None),
            P(DEV, "xh"),
            P("xh", DEV, None),
            P("xh", DEV),
            P(),
            P(),
            P(),
            P(),
        ),
        out_specs=P(DEV, "xh", None),
        check_vma=False,
    )
    return inner
```
